256 devices in a mesh: chan: 32 (over z, x_hi, core), tm: 8 (over x_lo, y).
Axes of the slice: x: 4 (x_hi: 2, x_lo: 2; x = x_hi * 2 + x_lo), y: 4, z: 8, core: 2. Of those that a mesh axis runs over, the one named last changes fastest.
Arguments:
- record: float32 [4096, 8192], P('chan', 'tm'), may hold values from -6 to 6
- alive: int32 [4096], P('chan'), may hold values 0 or 1
- taps: float32 [64], replicated, may hold values from -0.75 to 0.75
- pattern: int32 [256, 2], P(('chan', 'tm')), may hold values from 0 to 3
Outputs:
- correlations: float32 [256, 2, 16, 16, 1024], P(('chan', 'tm'))
The draws below stay inside these ranges and needn't reach their ends.
Inputs may be any that keep to these rules, and one draw needn't show every extreme that they name: `pattern`: partner blocks that lie past the last channel count as zeros.
All inputs are finite; a program needn't handle non-finite values. No bound on the sum of `alive` on one device may be relied on, other than what follows from the above.
Results may differ from the reference program's by a relative error of at most 0.0037.
Values may be sent and summed in bfloat16 or wider, within the bound.
A program may use at most 128 MiB of HBM per device.

```python
import math
import jax
import jax.numpy as jnp
from jax import lax

TAPS = 64
HALF_WIN = 256
LAG = 512
BLOCK = 16
PAIR_SPAN = 4
PAIRS = 2
CHANNELS = 4096
TIMES = 8192
BLOCKS = 256


def with_ends(values, own_key, low, largest):
    extent = values.shape
    spot = [jax.random.randint(jax.random.fold_in(own_key, axis), (), 0, extent[axis]) for axis in range(len(extent))]
    values = values.at[tuple(spot)].set(low)
    longest = extent.index(max(extent))
    spot[longest] = (spot[longest] + 1) % extent[longest]
    return values.at[tuple(spot)].set(largest)


def shard_levels(stream_key, shape, shards, low, high):
    def one(axis_at, shards_of):
        heights = jax.random.uniform(jax.random.fold_in(jax.random.fold_in(stream_key, 6), axis_at), (shards_of,), jnp.float32, low / len(shards), high / len(shards))
        return jnp.repeat(jnp.exp(heights), shape[axis_at] // shards_of).reshape((-1,) + (1,) * (len(shape) - axis_at - 1))

    factor_of = one(*shards[0])
    for cut in shards[1:]:
        factor_of = factor_of * one(*cut)
    return factor_of


def gaussian(own_key, dims, width, limit, shards=(), kind=jnp.bfloat16):
    array = jax.random.normal(own_key, dims, jnp.float32) * width
    if len(shards) > 0:
        array = shard_levels(own_key, dims, shards, -0.22, 0.18) * array
    return jnp.clip(array, min=-limit, max=limit).astype(kind)


def setup_inputs(seed: int = 0) -> dict:
    streams_of = jax.random.split(jax.random.key(seed), 5)
    return {
        "record": gaussian(streams_of[0], (CHANNELS, TIMES), 1.0, 6.0, ((0, 32), (1, 8)), jnp.float32),
        "alive": with_ends((jax.random.randint(streams_of[1], (CHANNELS,), 0, 16) < 15).astype(jnp.int32), jax.random.fold_in(streams_of[1], 1), 0, 1),
        "taps": gaussian(streams_of[2], (TAPS,), TAPS ** -0.5, 0.75, (), jnp.float32),
        "pattern": with_ends(jax.random.randint(streams_of[3], (BLOCKS, PAIRS), 0, PAIR_SPAN), jax.random.fold_in(streams_of[3], 1), 0, PAIR_SPAN - 1).astype(jnp.int32),
    }


def reference(record, alive, taps, pattern):
    lively = alive.astype(jnp.float32)[:, None]
    masked = record * lively
    rimmed = jnp.pad(masked, ((TAPS // 2, TAPS // 2), (0, 0)))
    filtered = jnp.zeros_like(record)
    for index in range(TAPS):
        filtered = filtered + taps[index] * rimmed[index:index + CHANNELS]
    filtered = lively * filtered
    padded = jnp.pad(jnp.abs(filtered), ((0, 0), (HALF_WIN, HALF_WIN)))
    window_sum = lax.reduce_window(padded, jnp.zeros((), padded.dtype), lax.add, (1, 2 * HALF_WIN + 1), (1, 1), 'VALID')
    level = window_sum / (2 * HALF_WIN + 1)
    normed = (filtered / (level + 1e-05)).astype(jnp.bfloat16)
    full_len = TIMES + 2 * LAG
    spectra = jnp.fft.rfft(normed.astype(jnp.float32), n=full_len, axis=1)
    reach_rows = (PAIR_SPAN - 1) * BLOCK
    spectra = jnp.concatenate([spectra, jnp.zeros((reach_rows, spectra.shape[1]), spectra.dtype)], 0)

    def one_block(inputs):
        index, offsets = inputs
        mine = lax.dynamic_slice_in_dim(spectra, index * BLOCK, BLOCK, 0)
        theirs = jnp.stack([lax.dynamic_slice_in_dim(spectra, (index + offsets[pair]) * BLOCK, BLOCK, 0) for pair in range(PAIRS)])
        cross = jnp.conj(mine)[None, :, None, :] * theirs[:, None, :, :]
        lagged = jnp.fft.irfft(cross, n=full_len, axis=-1)
        return jnp.concatenate([lagged[..., full_len - LAG:], lagged[..., :LAG]], -1)
    blocks_all = jnp.arange(BLOCKS).astype(jnp.int32)
    result = lax.map(one_block, (blocks_all, pattern.astype(jnp.int32)))
    return result * (1.0 / math.sqrt(TIMES))
```

```python
import math

import jax
import jax.numpy as jnp
from jax import lax
from jax.experimental import pallas as pl
from jax.experimental.pallas import tpu as pltpu
from jax.sharding import PartitionSpec as P

TAPS = 64
HALF_WIN = 256
LAG = 512
BLOCK = 16
PAIR_SPAN = 4
PAIRS = 2
T = 8192
KW = 8448
BW = KW + 896
KC = 2816


def extended_2(value, sides, width):
    for axis, dim in sides:
        devices, length = (lax.axis_size(axis), value.shape[dim])
        up = [(i, (i + 1) % devices) for i in range(devices - 1)]
        down = [(j, i) for i, j in up]
        last = lax.slice_in_dim(value, length - width, length, axis=dim)
        leading = lax.slice_in_dim(value, 0, width, axis=dim)
        before = lax.ppermute(last, axis, up)
        after = lax.ppermute(leading, axis, down)
        value = jnp.concatenate([before, value, after], axis=dim)
    return value


def from_behind(block, axis, distance):
    devices = range(lax.axis_size(axis))
    route = [(i - distance, i) for i in devices if i - distance in devices]
    return lax.ppermute(block, axis, route)


def band_matrix(taps, row_count):
    length = row_count + taps.shape[0]
    widened = jnp.concatenate([taps, jnp.zeros((row_count + 1,), taps.dtype)])
    repeated = jnp.broadcast_to(widened[None, :], (row_count, length + 1))
    return repeated.reshape(-1)[: row_count * length].reshape(row_count, length)


def running_level(magnitude):
    count, times = magnitude.shape
    width = 2 * HALF_WIN
    padded = jnp.pad(magnitude, ((0, 0), (HALF_WIN, HALF_WIN)))
    tiles = padded.reshape(count, times // width + 1, width)
    windows = jnp.concatenate([tiles[:, :-1], tiles[:, 1:]], -1)
    inner = jnp.arange(2 * width)[:, None]
    outer = jnp.arange(width)[None, :]
    boxcar = ((inner >= outer) & (inner <= outer + width)).astype(jnp.float32)
    summed = jnp.einsum(
        "cnx,xt->cnt",
        windows,
        boxcar,
        precision=lax.Precision.HIGHEST,
        preferred_element_type=jnp.float32,
    )
    return summed.reshape(count, times) / (width + 1)


def normalize(filtered):
    level = running_level(jnp.abs(filtered))
    return (filtered / (level + 1e-05)).astype(jnp.bfloat16)


def build_a(a32, a_sh):
    lane = lax.broadcasted_iota(jnp.int32,(8,128),1)
    sub = lax.broadcasted_iota(jnp.int32,(8,128),0)
    lo = lane >= sub
    hi = lane >= sub+8
    def col(u, prev):
        c0=pl.multiple_of(u*128,128)
        out=[]
        for i in range(16):
            x = jnp.broadcast_to(a32[i:i+1, pl.ds(c0,128)],(8,128))
            r0 = pltpu.roll(x,0,1,stride=1,stride_axis=0)
            r1 = pltpu.roll(x,8,1,stride=1,stride_axis=0)
            p0,p1=prev[i]
            y = jnp.concatenate([jnp.where(lo,r0,p0),jnp.where(hi,r1,p1)],0)
            a_sh[16*i:16*i+16, pl.ds(c0,128)] = y.astype(jnp.bfloat16)
            out.append((r0,r1))
        return tuple(out)
    z=jnp.zeros((8,128),jnp.float32)
    lax.fori_loop(0,KW//128,col,((z,z),)*16)

def build_b(bpad, b_sh):
    lane = lax.broadcasted_iota(jnp.int32,(32,128),1)
    def col(u,_):
        c0 = pl.multiple_of(u*128,128)
        x = bpad[:, pl.ds(c0,128)]
        y = bpad[:, pl.ds(pl.multiple_of(u*128+128,128),128)]
        b_sh[0:32, pl.ds(c0,128)] = x
        for q in range(1,8):
            s = 128-16*q
            w = jnp.where(lane < s, pltpu.roll(x.astype(jnp.float32),s,1), pltpu.roll(y.astype(jnp.float32),s,1))
            b_sh[32*q:32*q+32, pl.ds(c0,128)] = w.astype(jnp.bfloat16)
        return 0
    lax.fori_loop(0,BW//128,col,0,unroll=2)

def relayout(acc, o_ref, scale):
    lane = lax.broadcasted_iota(jnp.int32,(8,128),1)
    def one(g,_):
      qh=g
      for kj in range(8):
        k=kj//4; jh=(kj//2)%2; ih=kj%2
        xs=[acc[qh, 32*ql+k*16+jh*8:32*ql+k*16+jh*8+8, ih*128:ih*128+128]*scale for ql in range(8)]
        for b in (1,2,4):
            m = (lane//16)&b
            new=list(xs)
            for q in range(8):
                if q & b == 0:
                    x,y=xs[q],xs[q|b]
                    new[q]=jnp.where(m==0,x,pltpu.roll(y,16*b,1))
                    new[q|b]=jnp.where(m==0,pltpu.roll(x,128-16*b,1),y)
            xs=new
        for i in range(8):
            o_ref[k, ih*8+i, jh*8:jh*8+8, pl.ds(pl.multiple_of(qh*128,128),128)]=xs[i]
      return 0
    lax.fori_loop(0,8,one,0)

def kernel(pat, ext, o_ref, a32, a_sh, bpad, b_sh, acc):
    a32[:, :T] = ext[0:16, :].astype(jnp.float32)
    a32[:, T:] = jnp.zeros((16, KW - T), jnp.float32)
    build_a(a32, a_sh)
    bpad[:, :LAG] = jnp.zeros((32, LAG), jnp.bfloat16)
    bpad[:, LAG + T :] = jnp.zeros((32, BW + 128 - LAG - T), jnp.bfloat16)
    for k in range(PAIRS):
        first = pl.multiple_of(pat[0, k] * 16, 16)
        bpad[16 * k : 16 * k + 16, LAG : LAG + T] = ext[pl.ds(first, 16), :]
    build_b(bpad, b_sh)
    acc[...] = jnp.zeros_like(acc)

    def kouter(s, _):
        for qh in range(8):
            acc[qh] += lax.dot_general(
                b_sh[:, pl.ds(pl.multiple_of(s * KC + qh * 128, 128), KC)],
                a_sh[:, pl.ds(pl.multiple_of(s * KC, 128), KC)],
                (((1,), (1,)), ((), ())),
                preferred_element_type=jnp.float32,
            )
        return 0

    lax.fori_loop(0, KW // KC, kouter, 0)
    relayout(acc, o_ref, 1 / math.sqrt(T))


def correlate(pattern, ext):
    return pl.pallas_call(
        kernel,
        out_shape=jax.ShapeDtypeStruct((2, 16, 16, 1024), jnp.float32),
        in_specs=[
            pl.BlockSpec(memory_space=pltpu.SMEM),
            pl.BlockSpec(memory_space=pltpu.VMEM),
        ],
        out_specs=pl.BlockSpec(memory_space=pltpu.VMEM),
        scratch_shapes=[
            pltpu.VMEM((16, KW), jnp.float32),
            pltpu.VMEM((256, KW), jnp.bfloat16),
            pltpu.VMEM((32, BW + 128), jnp.bfloat16),
            pltpu.VMEM((256, BW), jnp.bfloat16),
            pltpu.VMEM((8, 256, 256), jnp.float32),
        ],
        compiler_params=pltpu.CompilerParams(vmem_limit_bytes=48 << 20),
        name="corr",
    )(pattern, ext)


def body(record, alive, taps, pattern):
    row_count, time_span = record.shape
    tm_count = lax.axis_size("tm")
    mine_count = row_count // tm_count
    reach_rows = (PAIR_SPAN - 1) * BLOCK
    lively = alive.astype(jnp.float32)[:, None]
    masked = record * lively
    rimmed = extended_2(masked, (("chan", 0),), TAPS // 2)
    filtered = lively * jnp.dot(
        band_matrix(taps, row_count),
        rimmed,
        precision=lax.Precision.HIGHEST,
        preferred_element_type=jnp.float32,
    )
    whole = lax.all_to_all(filtered, "tm", split_axis=0, concat_axis=1, tiled=True)
    normed = normalize(whole)
    needed = -(-reach_rows // mine_count)
    pieces = [normed]
    for step in range(1, needed + 1):
        pieces.append(from_behind(normed, ("chan", "tm"), -step))
    extended = jnp.concatenate(pieces, 0)
    return correlate(pattern, extended)[None]


def solution(mesh):
    placed = (P("chan", "tm"), P("chan"), P(), P(("chan", "tm"), None))
    return jax.shard_map(
        body,
        mesh=mesh,
        in_specs=placed,
        out_specs=P(("chan", "tm"), None, None, None, None),
        check_vma=False,
    )
```

```python
import math

import jax
import jax.numpy as jnp
from jax import lax
from jax.experimental import pallas as pl
from jax.experimental.pallas import tpu as pltpu
from jax.sharding import PartitionSpec as P

TAPS = 64
HALF_WIN = 256
LAG = 512
BLOCK = 16
PAIR_SPAN = 4
PAIRS = 2
T = 8192
KW = 8448
BW = KW + 896
KC = 2816


TM = 8
MESH = pl.DeviceIdType.MESH
DIRS = [(dc, dt) for dc in (-1, 0, 1) for dt in (-1, 0, 1) if (dc, dt) != (0, 0)]
ROWS = {-1: (32, 160, 32), 0: (32, 32, 128), 1: (128, 0, 32)}
COLS = {-1: (256, 1280, 256), 0: (256, 256, 1024), 1: (1024, 0, 256)}


def front_kernel(
    rec, alive, taps, pat, out, rim, nbuf, pack, pats,
    halo_send, halo_recv, pat_send, pat_recv, up_send, up_recv, send_sem, recv_sem,
):
    c = lax.axis_index("chan")
    t = lax.axis_index("tm")
    chans = lax.axis_size("chan")

    def inside(dc, dt):
        ok = jnp.bool_(True)
        if dc == -1:
            ok = ok & (c > 0)
        if dc == 1:
            ok = ok & (c < chans - 1)
        if dt == -1:
            ok = ok & (t > 0)
        if dt == 1:
            ok = ok & (t < TM - 1)
        return ok

    barrier = pltpu.get_barrier_semaphore()
    for d in range(1, TM):
        pl.semaphore_signal(barrier, inc=1, device_id=(c, lax.rem(t + d, TM)), device_id_type=MESH)
    for dc, dt in DIRS:
        if dc != 0:
            @pl.when(inside(dc, dt))
            def _():
                pl.semaphore_signal(barrier, inc=1, device_id=(c + dc, t + dt), device_id_type=MESH)

    eye = lax.broadcasted_iota(jnp.int32, (128, 128), 0) == lax.broadcasted_iota(jnp.int32, (128, 128), 1)
    row = jnp.broadcast_to(alive[...].astype(jnp.float32), (128, 128))
    lively = jnp.sum(jnp.where(eye, row, 0.0), axis=1, keepdims=True)
    rim[32:160, 256:1280] = rec[...] * lively
    pats[t, 0:8, :] = jnp.full((8, 128), pat[0, 0], jnp.int32)
    pats[t, 8:16, :] = jnp.full((8, 128), pat[0, 1], jnp.int32)

    @pl.when(c == 0)
    def _():
        rim[0:32, :] = jnp.zeros((32, 1536), jnp.float32)

    @pl.when(c == chans - 1)
    def _():
        rim[160:192, :] = jnp.zeros((32, 1536), jnp.float32)
        nbuf[128:176, :] = jnp.zeros((48, 1024), jnp.bfloat16)

    @pl.when(t == 0)
    def _():
        rim[:, 0:256] = jnp.zeros((192, 256), jnp.float32)

    @pl.when(t == TM - 1)
    def _():
        rim[:, 1280:1536] = jnp.zeros((192, 256), jnp.float32)

    peers = TM - 1 + jnp.where(c > 0, 1, 0) * (3 - jnp.where(t == 0, 1, 0) - jnp.where(t == TM - 1, 1, 0))
    peers = peers + jnp.where(c < chans - 1, 1, 0) * (3 - jnp.where(t == 0, 1, 0) - jnp.where(t == TM - 1, 1, 0))
    pl.semaphore_wait(barrier, peers)

    def halo(e, dc, dt, away=1):
        rs, rt, rn = ROWS[dc]
        cs, ct, cn = COLS[dt]
        return pltpu.make_async_remote_copy(
            src_ref=rim.at[pl.ds(rs, rn), pl.ds(cs, cn)],
            dst_ref=rim.at[pl.ds(rt, rn), pl.ds(ct, cn)],
            send_sem=halo_send.at[e], recv_sem=halo_recv.at[e],
            device_id=(c + away * dc, t + away * dt), device_id_type=MESH,
        )

    for e, (dc, dt) in enumerate(DIRS):
        @pl.when(inside(dc, dt))
        def _():
            halo(e, dc, dt).start()

    def pat_copy(d):
        return pltpu.make_async_remote_copy(
            src_ref=pats.at[t], dst_ref=pats.at[t], send_sem=pat_send.at[d], recv_sem=pat_recv.at[t],
            device_id=(c, lax.rem(t + d, TM)), device_id_type=MESH,
        )

    for d in range(1, TM):
        pat_copy(d).start()

    wide = jnp.concatenate([taps[...], jnp.zeros((1, 192), jnp.float32)], 1)
    band = pltpu.roll(jnp.broadcast_to(wide, (128, 256)), 0, 1, stride=1, stride_axis=0)[:, 0:192]
    inner = lax.broadcasted_iota(jnp.int32, (768, 256), 0)
    outer = lax.broadcasted_iota(jnp.int32, (768, 256), 1)
    boxcar = jnp.where((inner >= outer) & (inner <= outer + 512), 1.0, 0.0).astype(jnp.bfloat16)

    for e, (dc, dt) in enumerate(DIRS):
        @pl.when(inside(-dc, -dt))
        def _():
            halo(e, dc, dt, -1).wait_recv()

    filtered = lively * jnp.dot(
        band, rim[...], precision=lax.Precision.HIGHEST, preferred_element_type=jnp.float32
    )
    size = jnp.abs(filtered)
    high = size.astype(jnp.bfloat16)
    rest = size - high.astype(jnp.float32)
    mid = rest.astype(jnp.bfloat16)
    low = (rest - mid.astype(jnp.float32)).astype(jnp.bfloat16)
    for b in range(4):
        total = None
        for part in (high, mid, low):
            s = jnp.dot(part[:, 256 * b : 256 * b + 768], boxcar, preferred_element_type=jnp.float32)
            total = s if total is None else total + s
        level = total / (2 * HALF_WIN + 1)
        mine = filtered[:, 256 * b + 256 : 256 * b + 512]
        nbuf[0:128, 256 * b : 256 * b + 256] = (mine / (level + 1e-5)).astype(jnp.bfloat16)

    def up():
        return pltpu.make_async_remote_copy(
            src_ref=nbuf.at[pl.ds(0, 48), :], dst_ref=nbuf.at[pl.ds(128, 48), :],
            send_sem=up_send, recv_sem=up_recv, device_id=(c - 1, t), device_id_type=MESH,
        )

    @pl.when(c > 0)
    def _():
        up().start()

    def fill(dest, to):
        first = pl.multiple_of(dest * 16, 16)
        for j in range(8):
            cols = slice(128 * j, 128 * j + 128)
            blocks = [nbuf[pl.ds(pl.multiple_of(first + 16 * o, 16), 16), cols] for o in range(4)]
            to[0:16, cols] = blocks[0]
            for k in range(PAIRS):
                offset = pats[dest, 8 * k : 8 * k + 8, :]
                offset = jnp.concatenate([offset, offset], 0)
                chosen = None
                for o in range(4):
                    term = blocks[o].astype(jnp.float32)
                    chosen = term if o == 0 else jnp.where(offset == o, term, chosen)
                to[16 * k + 16 : 16 * k + 32, cols] = chosen.astype(jnp.bfloat16)

    def deliver(d):
        dest = lax.rem(t + d, TM)
        return pltpu.make_async_remote_copy(
            src_ref=pack.at[d], dst_ref=out.at[t], send_sem=send_sem.at[d], recv_sem=recv_sem.at[t],
            device_id=(c, dest), device_id_type=MESH,
        )

    for d in range(1, TM):
        src = lax.rem(t + d, TM)
        pltpu.make_async_remote_copy(
            src_ref=pats.at[src], dst_ref=pats.at[src], send_sem=pat_send.at[d], recv_sem=pat_recv.at[src],
            device_id=(c, src), device_id_type=MESH,
        ).wait_recv()

    for last in (False, True):
        if last:
            @pl.when(c < chans - 1)
            def _():
                up().wait_recv()
        for d in list(range(1, TM)) + [0]:
            dest = lax.rem(t + d, TM)
            @pl.when((dest >= 5) if last else (dest < 5))
            def _():
                if d == 0:
                    fill(dest, out.at[t])
                else:
                    fill(dest, pack.at[d])
                    deliver(d).start()

    for d in range(1, TM):
        src = lax.rem(t + d, TM)
        pltpu.make_async_remote_copy(
            src_ref=pack.at[d], dst_ref=out.at[src], send_sem=send_sem.at[d], recv_sem=recv_sem.at[src],
            device_id=(c, src), device_id_type=MESH,
        ).wait_recv()
    for d in range(1, TM):
        deliver(d).wait_send()
        pat_copy(d).wait_send()
    for e, (dc, dt) in enumerate(DIRS):
        @pl.when(inside(dc, dt))
        def _():
            halo(e, dc, dt).wait_send()

    @pl.when(c > 0)
    def _():
        up().wait_send()


def front(record, alive, taps, pattern):
    dma = pltpu.SemaphoreType.DMA
    return pl.pallas_call(
        front_kernel,
        out_shape=jax.ShapeDtypeStruct((TM, 48, 1024), jnp.bfloat16),
        in_specs=[pl.BlockSpec(memory_space=pltpu.VMEM)] * 3 + [pl.BlockSpec(memory_space=pltpu.SMEM)],
        out_specs=pl.BlockSpec(memory_space=pltpu.VMEM),
        scratch_shapes=[
            pltpu.VMEM((192, 1536), jnp.float32),
            pltpu.VMEM((176, 1024), jnp.bfloat16),
            pltpu.VMEM((TM, 48, 1024), jnp.bfloat16),
            pltpu.VMEM((TM, 16, 128), jnp.int32),
            dma((8,)), dma((8,)), dma((TM,)), dma((TM,)), dma(()), dma(()), dma((TM,)), dma((TM,)),
        ],
        compiler_params=pltpu.CompilerParams(
            collective_id=0, has_side_effects=True, vmem_limit_bytes=32 << 20
        ),
        name="front",
    )(record, alive.reshape(1, 128), taps.reshape(1, 64), pattern)


def build_a(a32, a_sh):
    lane = lax.broadcasted_iota(jnp.int32,(8,128),1)
    sub = lax.broadcasted_iota(jnp.int32,(8,128),0)
    lo = lane >= sub
    hi = lane >= sub+8
    def col(u, prev):
        c0=pl.multiple_of(u*128,128)
        out=[]
        for i in range(16):
            x = jnp.broadcast_to(a32[i:i+1, pl.ds(c0,128)],(8,128))
            r0 = pltpu.roll(x,0,1,stride=1,stride_axis=0)
            r1 = pltpu.roll(x,8,1,stride=1,stride_axis=0)
            p0,p1=prev[i]
            y = jnp.concatenate([jnp.where(lo,r0,p0),jnp.where(hi,r1,p1)],0)
            a_sh[16*i:16*i+16, pl.ds(c0,128)] = y.astype(jnp.bfloat16)
            out.append((r0,r1))
        return tuple(out)
    z=jnp.zeros((8,128),jnp.float32)
    lax.fori_loop(0,KW//128,col,((z,z),)*16)

def build_b(bpad, b_sh):
    lane = lax.broadcasted_iota(jnp.int32,(32,128),1)
    def col(u,_):
        c0 = pl.multiple_of(u*128,128)
        x = bpad[:, pl.ds(c0,128)]
        y = bpad[:, pl.ds(pl.multiple_of(u*128+128,128),128)]
        b_sh[0:32, pl.ds(c0,128)] = x
        for q in range(1,8):
            s = 128-16*q
            w = jnp.where(lane < s, pltpu.roll(x.astype(jnp.float32),s,1), pltpu.roll(y.astype(jnp.float32),s,1))
            b_sh[32*q:32*q+32, pl.ds(c0,128)] = w.astype(jnp.bfloat16)
        return 0
    lax.fori_loop(0,BW//128,col,0,unroll=2)

def relayout(acc, o_ref, scale):
    lane = lax.broadcasted_iota(jnp.int32,(8,128),1)
    def one(g,_):
      qh=g
      for kj in range(8):
        k=kj//4; jh=(kj//2)%2; ih=kj%2
        xs=[acc[qh, 32*ql+k*16+jh*8:32*ql+k*16+jh*8+8, ih*128:ih*128+128]*scale for ql in range(8)]
        for b in (1,2,4):
            m = (lane//16)&b
            new=list(xs)
            for q in range(8):
                if q & b == 0:
                    x,y=xs[q],xs[q|b]
                    new[q]=jnp.where(m==0,x,pltpu.roll(y,16*b,1))
                    new[q|b]=jnp.where(m==0,pltpu.roll(x,128-16*b,1),y)
            xs=new
        for i in range(8):
            o_ref[k, ih*8+i, jh*8:jh*8+8, pl.ds(pl.multiple_of(qh*128,128),128)]=xs[i]
      return 0
    lax.fori_loop(0,8,one,0)

def kernel(ext, o_ref, a32, a_sh, bpad, b_sh, acc):
    for s in range(8):
        a32[:, 1024 * s : 1024 * s + 1024] = ext[s, 0:16, :].astype(jnp.float32)
    a32[:, T:] = jnp.zeros((16, KW - T), jnp.float32)
    build_a(a32, a_sh)
    bpad[:, :LAG] = jnp.zeros((32, LAG), jnp.bfloat16)
    bpad[:, LAG + T :] = jnp.zeros((32, BW + 128 - LAG - T), jnp.bfloat16)
    for s in range(8):
        bpad[:, LAG + 1024 * s : LAG + 1024 * s + 1024] = ext[s, 16:48, :]
    build_b(bpad, b_sh)
    acc[...] = jnp.zeros_like(acc)

    def kouter(s, _):
        for qh in range(8):
            acc[qh] += lax.dot_general(
                b_sh[:, pl.ds(pl.multiple_of(s * KC + qh * 128, 128), KC)],
                a_sh[:, pl.ds(pl.multiple_of(s * KC, 128), KC)],
                (((1,), (1,)), ((), ())),
                preferred_element_type=jnp.float32,
            )
        return 0

    lax.fori_loop(0, KW // KC, kouter, 0)
    relayout(acc, o_ref, 1 / math.sqrt(T))


def correlate(ext):
    return pl.pallas_call(
        kernel,
        out_shape=jax.ShapeDtypeStruct((2, 16, 16, 1024), jnp.float32),
        in_specs=[
            pl.BlockSpec(memory_space=pltpu.VMEM),
        ],
        out_specs=pl.BlockSpec(memory_space=pltpu.VMEM),
        scratch_shapes=[
            pltpu.VMEM((16, KW), jnp.float32),
            pltpu.VMEM((256, KW), jnp.bfloat16),
            pltpu.VMEM((32, BW + 128), jnp.bfloat16),
            pltpu.VMEM((256, BW), jnp.bfloat16),
            pltpu.VMEM((8, 256, 256), jnp.float32),
        ],
        compiler_params=pltpu.CompilerParams(vmem_limit_bytes=48 << 20),
        name="corr",
    )(ext)


def body(record, alive, taps, pattern):
    return correlate(front(record, alive, taps, pattern))[None]


def solution(mesh):
    placed = (P("chan", "tm"), P("chan"), P(), P(("chan", "tm"), None))
    return jax.shard_map(
        body,
        mesh=mesh,
        in_specs=placed,
        out_specs=P(("chan", "tm"), None, None, None, None),
        check_vma=False,
    )
```

```python
import functools
import math

import jax
import jax.numpy as jnp
from jax import lax
from jax.experimental import pallas as pl
from jax.experimental.pallas import tpu as pltpu
from jax.sharding import PartitionSpec as P

TAPS = 64
HALF_WIN = 256
LAG = 512
BLOCK = 16
PAIR_SPAN = 4
PAIRS = 2
T = 8192


TM = 8
MESH = pl.DeviceIdType.MESH
ORDER = [(0, 0), (0, 1), (0, 3), (1, 0), (0, 2), (1, 1), (1, 3), (1, 2)]


def peer(t, dx, dy):
    return (t // 4 + dx) % 2 * 4 + (t % 4 + dy) % 4


def schedule():
    steps, needs = [], []
    for t in range(TM):
        rank = {peer(t, *d): r for r, d in enumerate(ORDER)}
        need = {low: max(rank.get(low, 0), rank.get(low + 1, 0)) for low in range(-1, TM)}
        order = sorted(need, key=lambda low: (need[low], low))
        steps.append([low + 1 for low in order])
        needs.append([need[low] for low in order])
    return steps, needs


def pick(values, index):
    out = jnp.int32(values[0])
    for n in range(1, len(values)):
        out = jnp.where(index == n, jnp.int32(values[n]), out)
    return out


def look_up(table, t, n):
    packed = [sum(row[m] * 9**k for k, row in enumerate(table)) for m in range(len(table[0]))]
    return pick(packed, n) // pick([9**k for k in range(TM)], t) % 9


DIRS = [(dc, dt) for dc in (-1, 0, 1) for dt in (-1, 0, 1) if (dc, dt) != (0, 0)]
ROWS = {-1: (32, 160, 32), 0: (32, 32, 128), 1: (128, 0, 32)}
COLS = {-1: (256, 1280, 256), 0: (256, 256, 1024), 1: (1024, 0, 256)}


def accumulate(low, high, acc, own, near, far, out, last):
    lane = lax.broadcasted_iota(jnp.int32, (8, 128), 1)
    sub = lax.broadcasted_iota(jnp.int32, (8, 128), 0)
    near[:, 0:640] = low[0:16, 384:1024].astype(jnp.float32)
    near[:, 640:1152] = high[0:16, 0:512].astype(jnp.float32)
    for i in range(BLOCK):
        before = None
        for u in range(9):
            x = jnp.broadcast_to(near[i : i + 1, 128 * u : 128 * u + 128], (8, 128))
            now = [pltpu.roll(x, 8 * h, 1, stride=1, stride_axis=0) for h in range(2)]
            if u > 0:
                y = [jnp.where(lane >= sub + 8 * h, now[h], before[h]) for h in range(2)]
                own[16 * i : 16 * i + 16, 128 * u - 128 : 128 * u] = jnp.concatenate(y, 0).astype(jnp.bfloat16)
            before = now
    both = jnp.concatenate([low[16:48, :], high[16:48, :]], 1)
    for ql in range(8):
        far[32 * ql : 32 * ql + 32, :] = both[:, 16 * ql : 16 * ql + 1920]

    def product(qh):
        return lax.dot_general(
            far[:, pl.ds(pl.multiple_of(128 * qh, 128), 1024)],
            own[...],
            (((1,), (1,)), ((), ())),
            preferred_element_type=jnp.float32,
        )

    for qh in range(8):
        acc[qh] += product(qh)

    @pl.when(last)
    def _():
        lax.fori_loop(0, 8, functools.partial(transpose, acc, out), 0)


def transpose(acc, out, qh, _):
    group = lax.broadcasted_iota(jnp.int32, (8, 128), 1) // 16
    for k in range(PAIRS):
        for jh in range(2):
            for ih in range(2):
                first = 16 * k + 8 * jh
                xs = []
                for ql in range(8):
                    x = acc[qh, 32 * ql + first : 32 * ql + first + 8, 128 * ih : 128 * ih + 128] * (1.0 / math.sqrt(T))
                    xs.append(pltpu.roll(x, 16 * ql, 1) if ql else x)
                xs = [xs[-m % 8] for m in range(8)]
                for bit in (1, 2, 4):
                    moved = group & bit != 0
                    xs = [jnp.where(moved, xs[(m - bit) % 8], xs[m]) for m in range(8)]
                for i in range(8):
                    y = pltpu.roll(xs[i], 128 - 16 * i, 1) if i else xs[i]
                    out[k, 8 * ih + i, 8 * jh : 8 * jh + 8, pl.ds(pl.multiple_of(128 * qh, 128), 128)] = y
    return 0


def front_kernel(
    rec_any, alive_any, taps_any, pat_any, out, acc, rec, alive, taps, pat, rim, nbuf, pack, pats, slots, own, near, far, filtered, sizes,
    arg_sem, halo_send, halo_recv, pat_send, pat_recv, up_send, up_recv, send_sem, recv_sem,
):
    c = lax.axis_index("chan")
    t = lax.axis_index("tm")
    chans = lax.axis_size("chan")

    def inside(dc, dt):
        ok = jnp.bool_(True)
        if dc == -1:
            ok = ok & (c > 0)
        if dc == 1:
            ok = ok & (c < chans - 1)
        if dt == -1:
            ok = ok & (t > 0)
        if dt == 1:
            ok = ok & (t < TM - 1)
        return ok

    arguments = [
        pltpu.make_async_copy(a, b, arg_sem.at[n])
        for n, (a, b) in enumerate(((rec_any, rec), (alive_any, alive), (taps_any, taps), (pat_any, pat)))
    ]
    for copy in arguments:
        copy.start()

    barrier = pltpu.get_barrier_semaphore()
    for d in range(1, TM):
        pl.semaphore_signal(barrier, inc=1, device_id=(c, lax.rem(t + d, TM)), device_id_type=MESH)
    for dc, dt in DIRS:
        if dc != 0:
            @pl.when(inside(dc, dt))
            def _():
                pl.semaphore_signal(barrier, inc=1, device_id=(c + dc, t + dt), device_id_type=MESH)

    slots[0] = jnp.zeros((48, 1024), jnp.bfloat16)
    slots[TM + 1] = jnp.zeros((48, 1024), jnp.bfloat16)
    for copy in arguments:
        copy.wait()

    eye = lax.broadcasted_iota(jnp.int32, (128, 128), 0) == lax.broadcasted_iota(jnp.int32, (128, 128), 1)
    row = jnp.broadcast_to(alive[...].astype(jnp.float32), (128, 128))
    lively = jnp.sum(jnp.where(eye, row, 0.0), axis=1, keepdims=True)
    rim[32:160, 256:1280] = rec[...] * lively
    pats[t, 0:8, :] = jnp.full((8, 128), pat[0, 0], jnp.int32)
    pats[t, 8:16, :] = jnp.full((8, 128), pat[0, 1], jnp.int32)

    @pl.when(c == 0)
    def _():
        rim[0:32, :] = jnp.zeros((32, 1536), jnp.float32)

    @pl.when(c == chans - 1)
    def _():
        rim[160:192, :] = jnp.zeros((32, 1536), jnp.float32)
        nbuf[128:176, :] = jnp.zeros((48, 1024), jnp.bfloat16)

    @pl.when(t == 0)
    def _():
        rim[:, 0:256] = jnp.zeros((192, 256), jnp.float32)

    @pl.when(t == TM - 1)
    def _():
        rim[:, 1280:1536] = jnp.zeros((192, 256), jnp.float32)

    peers = TM - 1 + jnp.where(c > 0, 1, 0) * (3 - jnp.where(t == 0, 1, 0) - jnp.where(t == TM - 1, 1, 0))
    peers = peers + jnp.where(c < chans - 1, 1, 0) * (3 - jnp.where(t == 0, 1, 0) - jnp.where(t == TM - 1, 1, 0))
    pl.semaphore_wait(barrier, peers)

    def halo(e, dc, dt, away=1):
        rs, rt, rn = ROWS[dc]
        cs, ct, cn = COLS[dt]
        return pltpu.make_async_remote_copy(
            src_ref=rim.at[pl.ds(rs, rn), pl.ds(cs, cn)],
            dst_ref=rim.at[pl.ds(rt, rn), pl.ds(ct, cn)],
            send_sem=halo_send.at[e], recv_sem=halo_recv.at[e],
            device_id=(c + away * dc, t + away * dt), device_id_type=MESH,
        )

    for e, (dc, dt) in enumerate(DIRS):
        @pl.when(inside(dc, dt))
        def _():
            halo(e, dc, dt).start()

    def pat_copy(d):
        return pltpu.make_async_remote_copy(
            src_ref=pats.at[t], dst_ref=pats.at[t], send_sem=pat_send.at[d], recv_sem=pat_recv.at[t],
            device_id=(c, lax.rem(t + d, TM)), device_id_type=MESH,
        )

    def send_pattern(d, _):
        pat_copy(d).start()
        return 0

    lax.fori_loop(1, TM, send_pattern, 0)

    acc[...] = jnp.zeros_like(acc)

    wide = jnp.concatenate([taps[...], jnp.zeros((1, 192), jnp.float32)], 1)
    band = pltpu.roll(jnp.broadcast_to(wide, (128, 256)), 0, 1, stride=1, stride_axis=0)[:, 0:192]
    inner = lax.broadcasted_iota(jnp.int32, (768, 256), 0)
    outer = lax.broadcasted_iota(jnp.int32, (768, 256), 1)
    boxcar = jnp.where((inner >= outer) & (inner <= outer + 512), 1.0, 0.0).astype(jnp.bfloat16)

    for e, (dc, dt) in enumerate(DIRS):
        @pl.when(inside(-dc, -dt))
        def _():
            halo(e, dc, dt, -1).wait_recv()

    def clean(b, _):
        cols = pl.ds(pl.multiple_of(256 * b, 256), 256)
        f = lively * jnp.dot(
            band, rim[:, cols], precision=lax.Precision.HIGHEST, preferred_element_type=jnp.float32
        )
        filtered[:, cols] = f
        rest = jnp.abs(f)
        for part in range(3):
            sizes[part, :, cols] = rest.astype(jnp.bfloat16)
            rest = rest - sizes[part, :, cols].astype(jnp.float32)
        return 0

    lax.fori_loop(0, 6, clean, 0)

    def scale(b, _):
        first = pl.multiple_of(256 * b, 256)
        total = None
        for part in range(3):
            s = jnp.dot(sizes[part, :, pl.ds(first, 768)], boxcar, preferred_element_type=jnp.float32)
            total = s if total is None else total + s
        level = total / (2 * HALF_WIN + 1)
        mine = filtered[:, pl.ds(first + 256, 256)]
        nbuf[0:128, pl.ds(first, 256)] = (mine / (level + 1e-5)).astype(jnp.bfloat16)
        return 0

    lax.fori_loop(0, 4, scale, 0)

    def up():
        return pltpu.make_async_remote_copy(
            src_ref=nbuf.at[pl.ds(0, 48), :], dst_ref=nbuf.at[pl.ds(128, 48), :],
            send_sem=up_send, recv_sem=up_recv, device_id=(c - 1, t), device_id_type=MESH,
        )

    @pl.when(c > 0)
    def _():
        up().start()

    def other(r):
        dx, dy = pick([d[0] for d in ORDER], r), pick([d[1] for d in ORDER], r)
        return lax.rem(t // 4 + dx, 2) * 4 + lax.rem(lax.rem(t, 4) + 4 - dy, 4)

    def source(r):
        dx, dy = pick([d[0] for d in ORDER], r), pick([d[1] for d in ORDER], r)
        return lax.rem(t // 4 + dx, 2) * 4 + lax.rem(lax.rem(t, 4) + dy, 4)

    def fill(dest, to):
        first = pl.multiple_of(dest * 16, 16)
        offsets = [jnp.concatenate([pats[dest, 8 * k : 8 * k + 8, :]] * 2, 0) for k in range(PAIRS)]
        for j in range(8):
            cols = slice(128 * j, 128 * j + 128)
            blocks = [nbuf[pl.ds(pl.multiple_of(first + 16 * o, 16), 16), cols] for o in range(4)]
            to[0:16, cols] = blocks[0]
            blocks = [block.astype(jnp.float32) for block in blocks]
            for k in range(PAIRS):
                chosen = blocks[0]
                for o in range(1, 4):
                    chosen = jnp.where(offsets[k] == o, blocks[o], chosen)
                to[16 * k + 16 : 16 * k + 32, cols] = chosen.astype(jnp.bfloat16)

    def deliver(r, dest):
        return pltpu.make_async_remote_copy(
            src_ref=pack.at[r], dst_ref=slots.at[t + 1], send_sem=send_sem.at[r], recv_sem=recv_sem.at[t],
            device_id=(c, dest), device_id_type=MESH,
        )

    def arrival(r):
        src = source(r)
        return pltpu.make_async_remote_copy(
            src_ref=pack.at[r], dst_ref=slots.at[src + 1], send_sem=send_sem.at[r], recv_sem=recv_sem.at[src],
            device_id=(c, src), device_id_type=MESH,
        )

    def await_pattern(d, _):
        src = lax.rem(t + d, TM)
        pltpu.make_async_remote_copy(
            src_ref=pats.at[src], dst_ref=pats.at[src], send_sem=pat_send.at[d], recv_sem=pat_recv.at[src],
            device_id=(c, src), device_id_type=MESH,
        ).wait_recv()
        return 0

    lax.fori_loop(1, TM, await_pattern, 0)

    def hand_out(n, _):
        r = lax.rem(n + 1, TM)
        dest = other(r)

        @pl.when((n == TM) & (c < chans - 1))
        def _():
            up().wait_recv()

        @pl.when((dest >= 5) == (n >= TM))
        def _():
            fill(dest, pack.at[r])

            @pl.when(r > 0)
            def _():
                deliver(r, dest).start()

            @pl.when(r == 0)
            def _():
                slots[t + 1] = pack[0]

        return 0

    lax.fori_loop(0, 2 * TM, hand_out, 0)

    steps, needs = schedule()

    def step(n, _):
        def take(r, _):
            arrival(r).wait_recv()
            return 0

        begin = jnp.where(n == 0, 0, look_up(needs, t, jnp.maximum(n - 1, 0)))
        lax.fori_loop(begin + 1, look_up(needs, t, n) + 1, take, 0)
        low = look_up(steps, t, n)
        accumulate(slots.at[low], slots.at[low + 1], acc, own, near, far, out, n == TM)
        return 0

    lax.fori_loop(0, TM + 1, step, 0)

    def finish(r, _):
        deliver(r, other(r)).wait_send()
        pat_copy(r).wait_send()
        return 0

    lax.fori_loop(1, TM, finish, 0)
    for e, (dc, dt) in enumerate(DIRS):
        @pl.when(inside(dc, dt))
        def _():
            halo(e, dc, dt).wait_send()

    @pl.when(c > 0)
    def _():
        up().wait_send()


def front(record, alive, taps, pattern):
    dma = pltpu.SemaphoreType.DMA
    return pl.pallas_call(
        front_kernel,
        out_shape=jax.ShapeDtypeStruct((PAIRS, BLOCK, BLOCK, 2 * LAG), jnp.float32),
        in_specs=[pl.BlockSpec(memory_space=pltpu.HBM)] * 4,
        out_specs=pl.BlockSpec(memory_space=pltpu.VMEM),
        scratch_shapes=[
            pltpu.VMEM((8, 256, 256), jnp.float32),
            pltpu.VMEM((128, 1024), jnp.float32),
            pltpu.VMEM((1, 128), jnp.int32),
            pltpu.VMEM((1, 64), jnp.float32),
            pltpu.SMEM((1, 2), jnp.int32),
            pltpu.VMEM((192, 1536), jnp.float32),
            pltpu.VMEM((176, 1024), jnp.bfloat16),
            pltpu.VMEM((TM, 48, 1024), jnp.bfloat16),
            pltpu.VMEM((TM, 16, 128), jnp.int32),
            pltpu.VMEM((TM + 2, 48, 1024), jnp.bfloat16),
            pltpu.VMEM((256, 1024), jnp.bfloat16),
            pltpu.VMEM((16, 1152), jnp.float32),
            pltpu.VMEM((256, 1920), jnp.bfloat16),
            pltpu.VMEM((128, 1536), jnp.float32),
            pltpu.VMEM((3, 128, 1536), jnp.bfloat16),
            dma((4,)), dma((8,)), dma((8,)), dma((TM,)), dma((TM,)), dma(()), dma(()), dma((TM,)), dma((TM,)),
        ],
        compiler_params=pltpu.CompilerParams(
            collective_id=0, has_side_effects=True, vmem_limit_bytes=32 << 20
        ),
        name="front",
    )(record, alive.reshape(1, 128), taps.reshape(1, 64), pattern)


def body(record, alive, taps, pattern):
    return front(record, alive, taps, pattern)[None]


def solution(mesh):
    placed = (P("chan", "tm"), P("chan"), P(), P(("chan", "tm"), None))
    return jax.shard_map(
        body,
        mesh=mesh,
        in_specs=placed,
        out_specs=P(("chan", "tm"), None, None, None, None),
        check_vma=False,
    )
```

```python
import functools
import math

import jax
import jax.numpy as jnp
from jax import lax
from jax.experimental import pallas as pl
from jax.experimental.pallas import tpu as pltpu
from jax.sharding import PartitionSpec as P

TAPS = 64
HALF_WIN = 256
LAG = 512
BLOCK = 16
PAIR_SPAN = 4
PAIRS = 2
T = 8192


TM = 8
MESH = pl.DeviceIdType.MESH
ORDER = [(0, 0), (0, 1), (0, 3), (1, 0), (0, 2), (1, 1), (1, 3), (1, 2)]


def peer(t, dx, dy):
    return (t // 4 + dx) % 2 * 4 + (t % 4 + dy) % 4


def schedule():
    steps, needs = [], []
    for t in range(TM):
        rank = {peer(t, *d): r for r, d in enumerate(ORDER)}
        need = {low: max(rank.get(low, 0), rank.get(low + 1, 0)) for low in range(-1, TM)}
        order = sorted(need, key=lambda low: (need[low], low))
        steps.append([low + 1 for low in order])
        needs.append([need[low] for low in order])
    return steps, needs


def pick(values, index):
    out = jnp.int32(values[0])
    for n in range(1, len(values)):
        out = jnp.where(index == n, jnp.int32(values[n]), out)
    return out


def look_up(table, t, n):
    packed = [sum(row[m] * 9**k for k, row in enumerate(table)) for m in range(len(table[0]))]
    return pick(packed, n) // pick([9**k for k in range(TM)], t) % 9


DIRS = [(dc, dt) for dc in (-1, 0, 1) for dt in (-1, 0, 1) if (dc, dt) != (0, 0)]
ROWS = {-1: (32, 160, 32), 0: (32, 32, 128), 1: (128, 0, 32)}
COLS = {-1: (256, 1280, 256), 0: (256, 256, 1024), 1: (1024, 0, 256)}


def accumulate(low, high, acc, own, near, far, out, last):
    lane = lax.broadcasted_iota(jnp.int32, (8, 128), 1)
    sub = lax.broadcasted_iota(jnp.int32, (8, 128), 0)
    near[:, 0:640] = low[0:16, 384:1024].astype(jnp.float32)
    near[:, 640:1152] = high[0:16, 0:512].astype(jnp.float32)
    for i in range(BLOCK):
        before = None
        for u in range(9):
            x = jnp.broadcast_to(near[i : i + 1, 128 * u : 128 * u + 128], (8, 128))
            now = [pltpu.roll(x, 8 * h, 1, stride=1, stride_axis=0) for h in range(2)]
            if u > 0:
                y = [jnp.where(lane >= sub + 8 * h, now[h], before[h]) for h in range(2)]
                own[16 * i : 16 * i + 16, 128 * u - 128 : 128 * u] = jnp.concatenate(y, 0).astype(jnp.bfloat16)
            before = now
    both = jnp.concatenate([low[16:48, :], high[16:48, :]], 1)
    for ql in range(8):
        far[32 * ql : 32 * ql + 32, :] = both[:, 16 * ql : 16 * ql + 1920]

    def product(qh):
        return lax.dot_general(
            far[:, pl.ds(pl.multiple_of(128 * qh, 128), 1024)],
            own[...],
            (((1,), (1,)), ((), ())),
            preferred_element_type=jnp.float32,
        )

    for qh in range(8):
        acc[qh] += product(qh)

    @pl.when(last)
    def _():
        lax.fori_loop(0, 8, functools.partial(transpose, acc, out), 0)


def transpose(acc, out, qh, _):
    group = lax.broadcasted_iota(jnp.int32, (8, 128), 1) // 16
    for k in range(PAIRS):
        for jh in range(2):
            for ih in range(2):
                first = 16 * k + 8 * jh
                xs = []
                for ql in range(8):
                    x = acc[qh, 32 * ql + first : 32 * ql + first + 8, 128 * ih : 128 * ih + 128] * (1.0 / math.sqrt(T))
                    xs.append(pltpu.roll(x, 16 * ql, 1) if ql else x)
                xs = [xs[-m % 8] for m in range(8)]
                for bit in (1, 2, 4):
                    moved = group & bit != 0
                    xs = [jnp.where(moved, xs[(m - bit) % 8], xs[m]) for m in range(8)]
                for i in range(8):
                    y = pltpu.roll(xs[i], 128 - 16 * i, 1) if i else xs[i]
                    out[k, 8 * ih + i, 8 * jh : 8 * jh + 8, pl.ds(pl.multiple_of(128 * qh, 128), 128)] = y
    return 0


def front_kernel(
    rec_any, alive_any, taps_any, pat_any, out, acc, rec, alive, taps, pat, rim, nbuf, pack, pats, slots, own, near, far, filtered, sizes,
    arg_sem, halo_send, halo_recv, pat_send, pat_recv, up_send, up_recv, send_sem, recv_sem,
):
    c = lax.axis_index("chan")
    t = lax.axis_index("tm")
    chans = lax.axis_size("chan")

    def inside(dc, dt):
        ok = jnp.bool_(True)
        if dc == -1:
            ok = ok & (c > 0)
        if dc == 1:
            ok = ok & (c < chans - 1)
        if dt == -1:
            ok = ok & (t > 0)
        if dt == 1:
            ok = ok & (t < TM - 1)
        return ok

    arguments = [
        pltpu.make_async_copy(a, b, arg_sem.at[n])
        for n, (a, b) in enumerate(((rec_any, rec), (alive_any, alive), (taps_any, taps), (pat_any, pat)))
    ]
    for copy in arguments:
        copy.start()

    barrier = pltpu.get_barrier_semaphore()
    for d in range(1, TM):
        pl.semaphore_signal(barrier, inc=1, device_id=(c, lax.rem(t + d, TM)), device_id_type=MESH)
    for dc, dt in DIRS:
        if dc != 0:
            @pl.when(inside(dc, dt))
            def _():
                pl.semaphore_signal(barrier, inc=1, device_id=(c + dc, t + dt), device_id_type=MESH)

    slots[0] = jnp.zeros((48, 1024), jnp.bfloat16)
    slots[TM + 1] = jnp.zeros((48, 1024), jnp.bfloat16)
    for copy in arguments:
        copy.wait()

    eye = lax.broadcasted_iota(jnp.int32, (128, 128), 0) == lax.broadcasted_iota(jnp.int32, (128, 128), 1)
    row = jnp.broadcast_to(alive[...].astype(jnp.float32), (128, 128))
    lively = jnp.sum(jnp.where(eye, row, 0.0), axis=1, keepdims=True)
    rim[32:160, 256:1280] = rec[...] * lively
    pats[t, 0:8, :] = jnp.full((8, 128), pat[0, 0], jnp.int32)
    pats[t, 8:16, :] = jnp.full((8, 128), pat[0, 1], jnp.int32)

    @pl.when(c == 0)
    def _():
        rim[0:32, :] = jnp.zeros((32, 1536), jnp.float32)

    @pl.when(c == chans - 1)
    def _():
        rim[160:192, :] = jnp.zeros((32, 1536), jnp.float32)
        nbuf[128:176, :] = jnp.zeros((48, 1024), jnp.bfloat16)

    @pl.when(t == 0)
    def _():
        rim[:, 0:256] = jnp.zeros((192, 256), jnp.float32)

    @pl.when(t == TM - 1)
    def _():
        rim[:, 1280:1536] = jnp.zeros((192, 256), jnp.float32)

    peers = TM - 1 + jnp.where(c > 0, 1, 0) * (3 - jnp.where(t == 0, 1, 0) - jnp.where(t == TM - 1, 1, 0))
    peers = peers + jnp.where(c < chans - 1, 1, 0) * (3 - jnp.where(t == 0, 1, 0) - jnp.where(t == TM - 1, 1, 0))
    pl.semaphore_wait(barrier, peers)

    def halo(e, dc, dt, away=1):
        rs, rt, rn = ROWS[dc]
        cs, ct, cn = COLS[dt]
        return pltpu.make_async_remote_copy(
            src_ref=rim.at[pl.ds(rs, rn), pl.ds(cs, cn)],
            dst_ref=rim.at[pl.ds(rt, rn), pl.ds(ct, cn)],
            send_sem=halo_send.at[e], recv_sem=halo_recv.at[e],
            device_id=(c + away * dc, t + away * dt), device_id_type=MESH,
        )

    for e, (dc, dt) in enumerate(DIRS):
        @pl.when(inside(dc, dt))
        def _():
            halo(e, dc, dt).start()

    def pat_copy(d):
        return pltpu.make_async_remote_copy(
            src_ref=pats.at[t], dst_ref=pats.at[t], send_sem=pat_send.at[d], recv_sem=pat_recv.at[t],
            device_id=(c, lax.rem(t + d, TM)), device_id_type=MESH,
        )

    def send_pattern(d, _):
        pat_copy(d).start()
        return 0

    lax.fori_loop(1, TM, send_pattern, 0)

    acc[...] = jnp.zeros_like(acc)

    wide = jnp.concatenate([taps[...], jnp.zeros((1, 192), jnp.float32)], 1)
    band = pltpu.roll(jnp.broadcast_to(wide, (128, 256)), 0, 1, stride=1, stride_axis=0)[:, 0:192]
    inner = lax.broadcasted_iota(jnp.int32, (768, 256), 0)
    outer = lax.broadcasted_iota(jnp.int32, (768, 256), 1)
    boxcar = jnp.where((inner >= outer) & (inner <= outer + 512), 1.0, 0.0).astype(jnp.bfloat16)

    def await_halo(sides):
        for e, (dc, dt) in enumerate(DIRS):
            if (dt != 0) == sides:
                @pl.when(inside(-dc, -dt))
                def _():
                    halo(e, dc, dt, -1).wait_recv()

    await_halo(False)

    def clean(b):
        cols = pl.ds(pl.multiple_of(256 * b, 256), 256)
        f = lively * jnp.dot(
            band, rim[:, cols], precision=lax.Precision.HIGHEST, preferred_element_type=jnp.float32
        )
        filtered[:, cols] = f
        rest = jnp.abs(f)
        for part in range(3):
            sizes[part, :, cols] = rest.astype(jnp.bfloat16)
            rest = rest - sizes[part, :, cols].astype(jnp.float32)

    def scale(b):
        first = pl.multiple_of(256 * b, 256)
        total = None
        for part in range(3):
            s = jnp.dot(sizes[part, :, pl.ds(first, 768)], boxcar, preferred_element_type=jnp.float32)
            total = s if total is None else total + s
        level = total / (2 * HALF_WIN + 1)
        mine = filtered[:, pl.ds(first + 256, 256)]
        nbuf[0:128, pl.ds(first, 256)] = (mine / (level + 1e-5)).astype(jnp.bfloat16)

    turns = [(1, 1), (1, 2), (1, 3), (1, 4), (0, 1), (0, 2), (1, 0), (1, 5), (0, 0), (0, 3)]

    def turn(n, _):
        block = pick([b for _, b in turns], n)
        cleans = pick([k for k, _ in turns], n)

        @pl.when(n == 6)
        def _():
            await_halo(True)

        @pl.when(cleans == 1)
        def _():
            clean(block)

        @pl.when(cleans == 0)
        def _():
            scale(block)

        return 0

    lax.fori_loop(0, len(turns), turn, 0)

    def up():
        return pltpu.make_async_remote_copy(
            src_ref=nbuf.at[pl.ds(0, 48), :], dst_ref=nbuf.at[pl.ds(128, 48), :],
            send_sem=up_send, recv_sem=up_recv, device_id=(c - 1, t), device_id_type=MESH,
        )

    @pl.when(c > 0)
    def _():
        up().start()

    def other(r):
        dx, dy = pick([d[0] for d in ORDER], r), pick([d[1] for d in ORDER], r)
        return lax.rem(t // 4 + dx, 2) * 4 + lax.rem(lax.rem(t, 4) + 4 - dy, 4)

    def source(r):
        dx, dy = pick([d[0] for d in ORDER], r), pick([d[1] for d in ORDER], r)
        return lax.rem(t // 4 + dx, 2) * 4 + lax.rem(lax.rem(t, 4) + dy, 4)

    def fill(dest, to):
        first = pl.multiple_of(dest * 16, 16)
        offsets = [jnp.concatenate([pats[dest, 8 * k : 8 * k + 8, :]] * 2, 0) for k in range(PAIRS)]
        for j in range(8):
            cols = slice(128 * j, 128 * j + 128)
            blocks = [nbuf[pl.ds(pl.multiple_of(first + 16 * o, 16), 16), cols] for o in range(4)]
            to[0:16, cols] = blocks[0]
            blocks = [block.astype(jnp.float32) for block in blocks]
            for k in range(PAIRS):
                chosen = blocks[0]
                for o in range(1, 4):
                    chosen = jnp.where(offsets[k] == o, blocks[o], chosen)
                to[16 * k + 16 : 16 * k + 32, cols] = chosen.astype(jnp.bfloat16)

    def deliver(r, dest):
        return pltpu.make_async_remote_copy(
            src_ref=pack.at[r], dst_ref=slots.at[t + 1], send_sem=send_sem.at[r], recv_sem=recv_sem.at[t],
            device_id=(c, dest), device_id_type=MESH,
        )

    def arrival(r):
        src = source(r)
        return pltpu.make_async_remote_copy(
            src_ref=pack.at[r], dst_ref=slots.at[src + 1], send_sem=send_sem.at[r], recv_sem=recv_sem.at[src],
            device_id=(c, src), device_id_type=MESH,
        )

    def await_pattern(d, _):
        src = lax.rem(t + d, TM)
        pltpu.make_async_remote_copy(
            src_ref=pats.at[src], dst_ref=pats.at[src], send_sem=pat_send.at[d], recv_sem=pat_recv.at[src],
            device_id=(c, src), device_id_type=MESH,
        ).wait_recv()
        return 0

    lax.fori_loop(1, TM, await_pattern, 0)

    def hand_out(n, _):
        r = pick([1, 2, 3, 1, 2, 3, 4, 5, 6, 7, 0], n)
        dest = other(r)

        @pl.when((n == 3) & (c < chans - 1))
        def _():
            up().wait_recv()

        @pl.when((n >= 6) | ((dest >= 5) == (n >= 3)))
        def _():
            fill(dest, pack.at[r])

            @pl.when(r > 0)
            def _():
                deliver(r, dest).start()

            @pl.when(r == 0)
            def _():
                slots[t + 1] = pack[0]

        return 0

    lax.fori_loop(0, 11, hand_out, 0)

    def follow(done, r):
        deliver(done, other(done)).wait_send()
        deliver(r, other(r)).start()

    steps, needs = schedule()

    def step(n, _):
        def take(r, _):
            arrival(r).wait_recv()
            return 0

        begin = jnp.where(n == 0, 0, look_up(needs, t, jnp.maximum(n - 1, 0)))
        lax.fori_loop(begin + 1, look_up(needs, t, n) + 1, take, 0)
        low = look_up(steps, t, n)
        accumulate(slots.at[low], slots.at[low + 1], acc, own, near, far, out, n == TM)
        return 0

    lax.fori_loop(0, TM + 1, step, 0)

    def finish(r, _):
        deliver(r, other(r)).wait_send()

        pat_copy(r).wait_send()
        return 0

    lax.fori_loop(1, TM, finish, 0)
    for e, (dc, dt) in enumerate(DIRS):
        @pl.when(inside(dc, dt))
        def _():
            halo(e, dc, dt).wait_send()

    @pl.when(c > 0)
    def _():
        up().wait_send()


def front(record, alive, taps, pattern):
    dma = pltpu.SemaphoreType.DMA
    return pl.pallas_call(
        front_kernel,
        out_shape=jax.ShapeDtypeStruct((PAIRS, BLOCK, BLOCK, 2 * LAG), jnp.float32),
        in_specs=[pl.BlockSpec(memory_space=pltpu.HBM)] * 4,
        out_specs=pl.BlockSpec(memory_space=pltpu.VMEM),
        scratch_shapes=[
            pltpu.VMEM((8, 256, 256), jnp.float32),
            pltpu.VMEM((128, 1024), jnp.float32),
            pltpu.VMEM((1, 128), jnp.int32),
            pltpu.VMEM((1, 64), jnp.float32),
            pltpu.SMEM((1, 2), jnp.int32),
            pltpu.VMEM((192, 1536), jnp.float32),
            pltpu.VMEM((176, 1024), jnp.bfloat16),
            pltpu.VMEM((TM, 48, 1024), jnp.bfloat16),
            pltpu.VMEM((TM, 16, 128), jnp.int32),
            pltpu.VMEM((TM + 2, 48, 1024), jnp.bfloat16),
            pltpu.VMEM((256, 1024), jnp.bfloat16),
            pltpu.VMEM((16, 1152), jnp.float32),
            pltpu.VMEM((256, 1920), jnp.bfloat16),
            pltpu.VMEM((128, 1536), jnp.float32),
            pltpu.VMEM((3, 128, 1536), jnp.bfloat16),
            dma((4,)), dma((8,)), dma((8,)), dma((TM,)), dma((TM,)), dma(()), dma(()), dma((TM,)), dma((TM,)),
        ],
        compiler_params=pltpu.CompilerParams(
            collective_id=0, has_side_effects=True, vmem_limit_bytes=32 << 20
        ),
        name="front",
    )(record, alive.reshape(1, 128), taps.reshape(1, 64), pattern)


def body(record, alive, taps, pattern):
    return front(record, alive, taps, pattern)[None]


def solution(mesh):
    placed = (P("chan", "tm"), P("chan"), P(), P(("chan", "tm"), None))
    return jax.shard_map(
        body,
        mesh=mesh,
        in_specs=placed,
        out_specs=P(("chan", "tm"), None, None, None, None),
        check_vma=False,
    )
```

```python
import functools
import math

import jax
import jax.numpy as jnp
from jax import lax
from jax.experimental import pallas as pl
from jax.experimental.pallas import tpu as pltpu
from jax.sharding import PartitionSpec as P

TAPS = 64
HALF_WIN = 256
LAG = 512
BLOCK = 16
PAIR_SPAN = 4
PAIRS = 2
T = 8192


TM = 8
MESH = pl.DeviceIdType.MESH
ORDER = [(0, 0), (0, 1), (0, 3), (1, 0), (0, 2), (1, 1), (1, 3), (1, 2)]


def peer(t, dx, dy):
    return (t // 4 + dx) % 2 * 4 + (t % 4 + dy) % 4


def schedule():
    steps, needs = [], []
    for t in range(TM):
        rank = {peer(t, *d): r for r, d in enumerate(ORDER)}
        need = {low: max(rank.get(low, 0), rank.get(low + 1, 0)) for low in range(-1, TM)}
        order = sorted(need, key=lambda low: (need[low], low))
        steps.append([low + 1 for low in order])
        needs.append([need[low] for low in order])
    return steps, needs


def pick(values, index):
    out = jnp.int32(values[0])
    for n in range(1, len(values)):
        out = jnp.where(index == n, jnp.int32(values[n]), out)
    return out


def look_up(table, t, n):
    packed = [sum(row[m] * 9**k for k, row in enumerate(table)) for m in range(len(table[0]))]
    return pick(packed, n) // pick([9**k for k in range(TM)], t) % 9


DIRS = [(dc, dt) for dc in (-1, 0, 1) for dt in (-1, 0, 1) if (dc, dt) != (0, 0)]
ROWS = {-1: (32, 160, 32), 0: (32, 32, 128), 1: (128, 0, 32)}
COLS = {-1: (256, 1280, 256), 0: (256, 256, 1024), 1: (1024, 0, 256)}


def accumulate(low, high, acc, own, near, far):
    lane = lax.broadcasted_iota(jnp.int32, (8, 128), 1)
    sub = lax.broadcasted_iota(jnp.int32, (8, 128), 0)
    near[:, 0:640] = low[0:16, 384:1024].astype(jnp.float32)
    near[:, 640:1152] = high[0:16, 0:512].astype(jnp.float32)
    for i in range(BLOCK):
        before = None
        for u in range(9):
            x = jnp.broadcast_to(near[i : i + 1, 128 * u : 128 * u + 128], (8, 128))
            now = [pltpu.roll(x, 8 * h, 1, stride=1, stride_axis=0) for h in range(2)]
            if u > 0:
                y = [jnp.where(lane >= sub + 8 * h, now[h], before[h]) for h in range(2)]
                own[16 * i : 16 * i + 16, 128 * u - 128 : 128 * u] = jnp.concatenate(y, 0).astype(jnp.bfloat16)
            before = now
    both = jnp.concatenate([low[16:48, :], high[16:48, :]], 1)
    for ql in range(8):
        far[32 * ql : 32 * ql + 32, :] = both[:, 16 * ql : 16 * ql + 1920]

    def product(qh):
        return lax.dot_general(
            far[:, pl.ds(pl.multiple_of(128 * qh, 128), 1024)],
            own[...],
            (((1,), (1,)), ((), ())),
            preferred_element_type=jnp.float32,
        )

    for qh in range(8):
        acc[qh] += product(qh)


def transpose(acc, out, qh, _):
    group = lax.broadcasted_iota(jnp.int32, (8, 128), 1) // 16
    for k in range(PAIRS):
        for jh in range(2):
            for ih in range(2):
                first = 16 * k + 8 * jh
                xs = []
                for ql in range(8):
                    x = acc[qh, 32 * ql + first : 32 * ql + first + 8, 128 * ih : 128 * ih + 128]
                    xs.append(pltpu.roll(x, 16 * ql, 1) if ql else x)
                xs = [xs[-m % 8] for m in range(8)]
                for bit in (1, 2, 4):
                    moved = group & bit != 0
                    xs = [jnp.where(moved, xs[(m - bit) % 8], xs[m]) for m in range(8)]
                for i in range(8):
                    y = pltpu.roll(xs[i], 128 - 16 * i, 1) if i else xs[i]
                    out[k, 8 * ih + i, 8 * jh : 8 * jh + 8, pl.ds(pl.multiple_of(128 * qh, 128), 128)] = y
    return 0


def front_kernel(
    rec_any, alive_any, taps_any, pat_any, final, acc, out, rec, alive, taps, pat, rim, nbuf, pack, pats, slots, own, near, far, filtered, sizes,
    out_sem, arg_sem, halo_send, halo_recv, pat_send, pat_recv, up_send, up_recv, send_sem, recv_sem,
):
    c = lax.axis_index("chan")
    t = lax.axis_index("tm")
    chans = lax.axis_size("chan")

    def inside(dc, dt):
        ok = jnp.bool_(True)
        if dc == -1:
            ok = ok & (c > 0)
        if dc == 1:
            ok = ok & (c < chans - 1)
        if dt == -1:
            ok = ok & (t > 0)
        if dt == 1:
            ok = ok & (t < TM - 1)
        return ok

    arguments = [
        pltpu.make_async_copy(a, b, arg_sem.at[n])
        for n, (a, b) in enumerate(((rec_any, rec), (alive_any, alive), (taps_any, taps), (pat_any, pat)))
    ]
    for copy in arguments:
        copy.start()

    barrier = pltpu.get_barrier_semaphore()
    for d in range(1, TM):
        pl.semaphore_signal(barrier, inc=1, device_id=(c, lax.rem(t + d, TM)), device_id_type=MESH)
    for dc, dt in DIRS:
        if dc != 0:
            @pl.when(inside(dc, dt))
            def _():
                pl.semaphore_signal(barrier, inc=1, device_id=(c + dc, t + dt), device_id_type=MESH)

    slots[0] = jnp.zeros((48, 1024), jnp.bfloat16)
    slots[TM + 1] = jnp.zeros((48, 1024), jnp.bfloat16)
    for copy in arguments:
        copy.wait()

    eye = lax.broadcasted_iota(jnp.int32, (128, 128), 0) == lax.broadcasted_iota(jnp.int32, (128, 128), 1)
    row = jnp.broadcast_to(alive[...].astype(jnp.float32), (128, 128))
    lively = jnp.sum(jnp.where(eye, row, 0.0), axis=1, keepdims=True)
    rim[32:160, 256:1280] = rec[...] * lively
    pats[t, 0:8, :] = jnp.full((8, 128), pat[0, 0], jnp.int32)
    pats[t, 8:16, :] = jnp.full((8, 128), pat[0, 1], jnp.int32)

    @pl.when(c == 0)
    def _():
        rim[0:32, :] = jnp.zeros((32, 1536), jnp.float32)

    @pl.when(c == chans - 1)
    def _():
        rim[160:192, :] = jnp.zeros((32, 1536), jnp.float32)
        nbuf[128:176, :] = jnp.zeros((48, 1024), jnp.bfloat16)

    @pl.when(t == 0)
    def _():
        rim[:, 0:256] = jnp.zeros((192, 256), jnp.float32)

    @pl.when(t == TM - 1)
    def _():
        rim[:, 1280:1536] = jnp.zeros((192, 256), jnp.float32)

    peers = TM - 1 + jnp.where(c > 0, 1, 0) * (3 - jnp.where(t == 0, 1, 0) - jnp.where(t == TM - 1, 1, 0))
    peers = peers + jnp.where(c < chans - 1, 1, 0) * (3 - jnp.where(t == 0, 1, 0) - jnp.where(t == TM - 1, 1, 0))
    pl.semaphore_wait(barrier, peers)

    def halo(e, dc, dt, away=1):
        rs, rt, rn = ROWS[dc]
        cs, ct, cn = COLS[dt]
        return pltpu.make_async_remote_copy(
            src_ref=rim.at[pl.ds(rs, rn), pl.ds(cs, cn)],
            dst_ref=rim.at[pl.ds(rt, rn), pl.ds(ct, cn)],
            send_sem=halo_send.at[e], recv_sem=halo_recv.at[e],
            device_id=(c + away * dc, t + away * dt), device_id_type=MESH,
        )

    for e, (dc, dt) in enumerate(DIRS):
        @pl.when(inside(dc, dt))
        def _():
            halo(e, dc, dt).start()

    def pat_copy(d):
        return pltpu.make_async_remote_copy(
            src_ref=pats.at[t], dst_ref=pats.at[t], send_sem=pat_send.at[d], recv_sem=pat_recv.at[t],
            device_id=(c, lax.rem(t + d, TM)), device_id_type=MESH,
        )

    def send_pattern(d, _):
        pat_copy(d).start()
        return 0

    lax.fori_loop(1, TM, send_pattern, 0)

    acc[...] = jnp.zeros_like(acc)

    wide = jnp.concatenate([taps[...], jnp.zeros((1, 192), jnp.float32)], 1)
    band = pltpu.roll(jnp.broadcast_to(wide, (128, 256)), 0, 1, stride=1, stride_axis=0)[:, 0:192]
    inner = lax.broadcasted_iota(jnp.int32, (768, 256), 0)
    outer = lax.broadcasted_iota(jnp.int32, (768, 256), 1)
    boxcar = jnp.where((inner >= outer) & (inner <= outer + 512), 1.0, 0.0).astype(jnp.bfloat16)

    def await_halo(sides):
        for e, (dc, dt) in enumerate(DIRS):
            if (dt != 0) == sides:
                @pl.when(inside(-dc, -dt))
                def _():
                    halo(e, dc, dt, -1).wait_recv()

    await_halo(False)

    def clean(b):
        cols = pl.ds(pl.multiple_of(256 * b, 256), 256)
        f = lively * jnp.dot(
            band, rim[:, cols], precision=lax.Precision.HIGHEST, preferred_element_type=jnp.float32
        )
        filtered[:, cols] = f
        rest = jnp.abs(f)
        for part in range(3):
            sizes[part, :, cols] = rest.astype(jnp.bfloat16)
            rest = rest - sizes[part, :, cols].astype(jnp.float32)

    def scale(b):
        first = pl.multiple_of(256 * b, 256)
        total = None
        for part in range(3):
            s = jnp.dot(sizes[part, :, pl.ds(first, 768)], boxcar, preferred_element_type=jnp.float32)
            total = s if total is None else total + s
        level = total / (2 * HALF_WIN + 1)
        mine = filtered[:, pl.ds(first + 256, 256)]
        nbuf[0:128, pl.ds(first, 256)] = (mine / (level + 1e-5)).astype(jnp.bfloat16)

    def up(piece):
        cols = pl.ds(*((256, 512), (0, 256), (768, 256))[piece])
        return pltpu.make_async_remote_copy(
            src_ref=nbuf.at[pl.ds(0, 48), cols], dst_ref=nbuf.at[pl.ds(128, 48), cols],
            send_sem=up_send.at[piece], recv_sem=up_recv.at[piece], device_id=(c - 1, t), device_id_type=MESH,
        )

    def up_start(piece):
        @pl.when(c > 0)
        def _():
            up(piece).start()

    turns = [(1, 1), (1, 2), (1, 3), (1, 4), (0, 1), (0, 2), (1, 0), (1, 5), (0, 0), (0, 3)]

    def turn(n, _):
        block = pick([b for _, b in turns], n)
        cleans = pick([k for k, _ in turns], n)

        @pl.when(n == 6)
        def _():
            up_start(0)
            await_halo(True)

        @pl.when(cleans == 1)
        def _():
            clean(block)

        @pl.when(cleans == 0)
        def _():
            scale(block)

        return 0

    lax.fori_loop(0, len(turns), turn, 0)

    up_start(1)
    up_start(2)

    def other(r):
        dx, dy = pick([d[0] for d in ORDER], r), pick([d[1] for d in ORDER], r)
        return lax.rem(t // 4 + dx, 2) * 4 + lax.rem(lax.rem(t, 4) + 4 - dy, 4)

    def source(r):
        dx, dy = pick([d[0] for d in ORDER], r), pick([d[1] for d in ORDER], r)
        return lax.rem(t // 4 + dx, 2) * 4 + lax.rem(lax.rem(t, 4) + dy, 4)

    def fill(dest, to):
        first = pl.multiple_of(dest * 16, 16)
        offsets = [jnp.concatenate([pats[dest, 8 * k : 8 * k + 8, :]] * 2, 0) for k in range(PAIRS)]
        for j in range(8):
            cols = slice(128 * j, 128 * j + 128)
            blocks = [nbuf[pl.ds(pl.multiple_of(first + 16 * o, 16), 16), cols] for o in range(4)]
            to[0:16, cols] = blocks[0]
            blocks = [block.astype(jnp.float32) for block in blocks]
            for k in range(PAIRS):
                chosen = blocks[0]
                for o in range(1, 4):
                    chosen = jnp.where(offsets[k] == o, blocks[o], chosen)
                to[16 * k + 16 : 16 * k + 32, cols] = chosen.astype(jnp.bfloat16)

    def deliver(r, dest):
        return pltpu.make_async_remote_copy(
            src_ref=pack.at[r], dst_ref=slots.at[t + 1], send_sem=send_sem.at[r], recv_sem=recv_sem.at[t],
            device_id=(c, dest), device_id_type=MESH,
        )

    def arrival(r):
        src = source(r)
        return pltpu.make_async_remote_copy(
            src_ref=pack.at[r], dst_ref=slots.at[src + 1], send_sem=send_sem.at[r], recv_sem=recv_sem.at[src],
            device_id=(c, src), device_id_type=MESH,
        )

    def await_pattern(d, _):
        src = lax.rem(t + d, TM)
        pltpu.make_async_remote_copy(
            src_ref=pats.at[src], dst_ref=pats.at[src], send_sem=pat_send.at[d], recv_sem=pat_recv.at[src],
            device_id=(c, src), device_id_type=MESH,
        ).wait_recv()
        return 0

    lax.fori_loop(1, TM, await_pattern, 0)

    def hand_out(n, _):
        r = pick([1, 2, 3, 1, 2, 3, 4, 5, 6, 7, 0], n)
        dest = other(r)

        @pl.when((n == 3) & (c < chans - 1))
        def _():
            for piece in range(3):
                up(piece).wait_recv()

        @pl.when((n >= 6) | ((dest >= 5) == (n >= 3)))
        def _():
            fill(dest, pack.at[r])

            @pl.when(r > 0)
            def _():
                deliver(r, dest).start()

            @pl.when(r == 0)
            def _():
                slots[t + 1] = pack[0]

        return 0

    lax.fori_loop(0, 11, hand_out, 0)

    def follow(done, r):
        deliver(done, other(done)).wait_send()
        deliver(r, other(r)).start()

    steps, needs = schedule()

    def step(n, _):
        def take(r, _):
            arrival(r).wait_recv()
            return 0

        begin = jnp.where(n == 0, 0, look_up(needs, t, jnp.maximum(n - 1, 0)))
        lax.fori_loop(begin + 1, look_up(needs, t, n) + 1, take, 0)
        low = look_up(steps, t, n)
        accumulate(slots.at[low], slots.at[low + 1], acc, own, near, far)
        return 0

    lax.fori_loop(0, TM + 1, step, 0)

    def put(qh):
        cols = pl.ds(pl.multiple_of(128 * qh, 128), 128)
        return pltpu.make_async_copy(out.at[:, :, :, cols], final.at[:, :, :, cols], out_sem.at[qh])

    def turn_over(qh, _):
        transpose(acc, out, qh, 0)
        put(qh).start()
        return 0

    def written(qh, _):
        put(qh).wait()
        return 0

    lax.fori_loop(0, 8, turn_over, 0)

    def finish(r, _):
        deliver(r, other(r)).wait_send()

        pat_copy(r).wait_send()
        return 0

    lax.fori_loop(1, TM, finish, 0)
    for e, (dc, dt) in enumerate(DIRS):
        @pl.when(inside(dc, dt))
        def _():
            halo(e, dc, dt).wait_send()

    @pl.when(c > 0)
    def _():
        for piece in range(3):
            up(piece).wait_send()

    lax.fori_loop(0, 8, written, 0)


def front(record, alive, taps, pattern):
    dma = pltpu.SemaphoreType.DMA
    return pl.pallas_call(
        front_kernel,
        out_shape=jax.ShapeDtypeStruct((PAIRS, BLOCK, BLOCK, 2 * LAG), jnp.float32),
        in_specs=[pl.BlockSpec(memory_space=pltpu.HBM)] * 4,
        out_specs=pl.BlockSpec(memory_space=pl.ANY),
        scratch_shapes=[
            pltpu.VMEM((8, 256, 256), jnp.float32),
            pltpu.VMEM((PAIRS, BLOCK, BLOCK, 2 * LAG), jnp.float32),
            pltpu.VMEM((128, 1024), jnp.float32),
            pltpu.VMEM((1, 128), jnp.int32),
            pltpu.VMEM((1, 64), jnp.float32),
            pltpu.SMEM((1, 2), jnp.int32),
            pltpu.VMEM((192, 1536), jnp.float32),
            pltpu.VMEM((176, 1024), jnp.bfloat16),
            pltpu.VMEM((TM, 48, 1024), jnp.bfloat16),
            pltpu.VMEM((TM, 16, 128), jnp.int32),
            pltpu.VMEM((TM + 2, 48, 1024), jnp.bfloat16),
            pltpu.VMEM((256, 1024), jnp.bfloat16),
            pltpu.VMEM((16, 1152), jnp.float32),
            pltpu.VMEM((256, 1920), jnp.bfloat16),
            pltpu.VMEM((128, 1536), jnp.float32),
            pltpu.VMEM((3, 128, 1536), jnp.bfloat16),
            dma((8,)), dma((4,)), dma((8,)), dma((8,)), dma((TM,)), dma((TM,)), dma((3,)), dma((3,)), dma((TM,)), dma((TM,)),
        ],
        compiler_params=pltpu.CompilerParams(
            collective_id=0, has_side_effects=True, vmem_limit_bytes=60 << 20
        ),
        name="front",
    )(record, alive.reshape(1, 128), taps.reshape(1, 64), pattern)


def body(record, alive, taps, pattern):
    return front(record, alive, taps, pattern)[None] * (1.0 / math.sqrt(T))


def solution(mesh):
    placed = (P("chan", "tm"), P("chan"), P(), P(("chan", "tm"), None))
    return jax.shard_map(
        body,
        mesh=mesh,
        in_specs=placed,
        out_specs=P(("chan", "tm"), None, None, None, None),
        check_vma=False,
    )
```

```python
import functools
import math

import jax
import jax.numpy as jnp
from jax import lax
from jax.experimental import pallas as pl
from jax.experimental.pallas import tpu as pltpu
from jax.sharding import PartitionSpec as P

TAPS = 64
HALF_WIN = 256
LAG = 512
BLOCK = 16
PAIR_SPAN = 4
PAIRS = 2
T = 8192


TM = 8
MESH = pl.DeviceIdType.MESH
ORDER = [(0, 0), (0, 1), (0, 3), (1, 0), (0, 2), (1, 1), (1, 3), (1, 2)]


def peer(t, dx, dy):
    return (t // 4 + dx) % 2 * 4 + (t % 4 + dy) % 4


def schedule():
    steps, needs = [], []
    for t in range(TM):
        rank = {peer(t, *d): r for r, d in enumerate(ORDER)}
        need = {low: max(rank.get(low, 0), rank.get(low + 1, 0)) for low in range(-1, TM)}
        order = sorted(need, key=lambda low: (need[low], low))
        steps.append([low + 1 for low in order])
        needs.append([need[low] for low in order])
    return steps, needs


def pick(values, index):
    out = jnp.int32(values[0])
    for n in range(1, len(values)):
        out = jnp.where(index == n, jnp.int32(values[n]), out)
    return out


def look_up(table, t, n):
    packed = [sum(row[m] * 9**k for k, row in enumerate(table)) for m in range(len(table[0]))]
    return pick(packed, n) // pick([9**k for k in range(TM)], t) % 9


DIRS = [(dc, dt) for dc in (-1, 0, 1) for dt in (-1, 0, 1) if (dc, dt) != (0, 0)]
ROWS = {-1: (32, 160, 32), 0: (32, 32, 128), 1: (128, 0, 32)}
COLS = {-1: (256, 1280, 256), 0: (256, 256, 1024), 1: (1024, 0, 256)}


def accumulate(low, high, acc, own, near, far):
    lane = lax.broadcasted_iota(jnp.int32, (8, 128), 1)
    sub = lax.broadcasted_iota(jnp.int32, (8, 128), 0)
    near[:, 0:640] = low[0:16, 384:1024].astype(jnp.float32)
    near[:, 640:1152] = high[0:16, 0:512].astype(jnp.float32)
    for i in range(BLOCK):
        before = None
        for u in range(9):
            x = jnp.broadcast_to(near[i : i + 1, 128 * u : 128 * u + 128], (8, 128))
            now = [pltpu.roll(x, 8 * h, 1, stride=1, stride_axis=0) for h in range(2)]
            if u > 0:
                y = [jnp.where(lane >= sub + 8 * h, now[h], before[h]) for h in range(2)]
                own[16 * i : 16 * i + 16, 128 * u - 128 : 128 * u] = jnp.concatenate(y, 0).astype(jnp.bfloat16)
            before = now
    both = jnp.concatenate([low[16:48, :], high[16:48, :]], 1)
    for ql in range(8):
        far[32 * ql : 32 * ql + 32, :] = both[:, 16 * ql : 16 * ql + 1920]

    def product(qh):
        return lax.dot_general(
            far[:, pl.ds(pl.multiple_of(128 * qh, 128), 1024)],
            own[...],
            (((1,), (1,)), ((), ())),
            preferred_element_type=jnp.float32,
        )

    for qh in range(8):
        acc[qh] += product(qh)


def transpose(acc, out, qh, _):
    group = lax.broadcasted_iota(jnp.int32, (8, 128), 1) // 16
    for k in range(PAIRS):
        for jh in range(2):
            for ih in range(2):
                first = 16 * k + 8 * jh
                xs = []
                for ql in range(8):
                    x = acc[qh, 32 * ql + first : 32 * ql + first + 8, 128 * ih : 128 * ih + 128]
                    xs.append(pltpu.roll(x, 16 * ql, 1) if ql else x)
                xs = [xs[-m % 8] for m in range(8)]
                for bit in (1, 2, 4):
                    moved = group & bit != 0
                    xs = [jnp.where(moved, xs[(m - bit) % 8], xs[m]) for m in range(8)]
                for i in range(8):
                    y = pltpu.roll(xs[i], 128 - 16 * i, 1) if i else xs[i]
                    out[k, 8 * ih + i, 8 * jh : 8 * jh + 8, pl.ds(pl.multiple_of(128 * qh, 128), 128)] = y
    return 0


def front_kernel(
    rec_any, alive_any, taps_any, pat_any, final, acc, out, rec, alive, taps, pat, rim, nbuf, pack, pats, slots, own, near, far, filtered, sizes,
    out_sem, arg_sem, halo_send, halo_recv, pat_send, pat_recv, up_send, up_recv, send_sem, recv_sem,
):
    c = lax.axis_index("chan")
    t = lax.axis_index("tm")
    chans = lax.axis_size("chan")

    def inside(dc, dt):
        ok = jnp.bool_(True)
        if dc == -1:
            ok = ok & (c > 0)
        if dc == 1:
            ok = ok & (c < chans - 1)
        if dt == -1:
            ok = ok & (t > 0)
        if dt == 1:
            ok = ok & (t < TM - 1)
        return ok

    arguments = [
        pltpu.make_async_copy(a, b, arg_sem.at[n])
        for n, (a, b) in enumerate(((rec_any, rec), (alive_any, alive), (taps_any, taps), (pat_any, pat)))
    ]
    for copy in arguments:
        copy.start()

    barrier = pltpu.get_barrier_semaphore()
    for d in range(1, TM):
        pl.semaphore_signal(barrier, inc=1, device_id=(c, lax.rem(t + d, TM)), device_id_type=MESH)
    for dc, dt in DIRS:
        if dc != 0:
            @pl.when(inside(dc, dt))
            def _():
                pl.semaphore_signal(barrier, inc=1, device_id=(c + dc, t + dt), device_id_type=MESH)

    slots[0] = jnp.zeros((48, 1024), jnp.bfloat16)
    slots[TM + 1] = jnp.zeros((48, 1024), jnp.bfloat16)
    for copy in arguments:
        copy.wait()

    eye = lax.broadcasted_iota(jnp.int32, (128, 128), 0) == lax.broadcasted_iota(jnp.int32, (128, 128), 1)
    row = jnp.broadcast_to(alive[...].astype(jnp.float32), (128, 128))
    lively = jnp.sum(jnp.where(eye, row, 0.0), axis=1, keepdims=True)
    rim[32:160, 256:1280] = rec[...] * lively
    pats[t, 0:8, :] = jnp.full((8, 128), pat[0, 0], jnp.int32)
    pats[t, 8:16, :] = jnp.full((8, 128), pat[0, 1], jnp.int32)

    @pl.when(c == 0)
    def _():
        rim[0:32, :] = jnp.zeros((32, 1536), jnp.float32)

    @pl.when(c == chans - 1)
    def _():
        rim[160:192, :] = jnp.zeros((32, 1536), jnp.float32)
        nbuf[128:176, :] = jnp.zeros((48, 1024), jnp.bfloat16)

    @pl.when(t == 0)
    def _():
        rim[:, 0:256] = jnp.zeros((192, 256), jnp.float32)

    @pl.when(t == TM - 1)
    def _():
        rim[:, 1280:1536] = jnp.zeros((192, 256), jnp.float32)

    peers = TM - 1 + jnp.where(c > 0, 1, 0) * (3 - jnp.where(t == 0, 1, 0) - jnp.where(t == TM - 1, 1, 0))
    peers = peers + jnp.where(c < chans - 1, 1, 0) * (3 - jnp.where(t == 0, 1, 0) - jnp.where(t == TM - 1, 1, 0))
    pl.semaphore_wait(barrier, peers)

    def halo(e, dc, dt, away=1):
        rs, rt, rn = ROWS[dc]
        cs, ct, cn = COLS[dt]
        return pltpu.make_async_remote_copy(
            src_ref=rim.at[pl.ds(rs, rn), pl.ds(cs, cn)],
            dst_ref=rim.at[pl.ds(rt, rn), pl.ds(ct, cn)],
            send_sem=halo_send.at[e], recv_sem=halo_recv.at[e],
            device_id=(c + away * dc, t + away * dt), device_id_type=MESH,
        )

    for e, (dc, dt) in enumerate(DIRS):
        @pl.when(inside(dc, dt))
        def _():
            halo(e, dc, dt).start()

    def pat_copy(d):
        return pltpu.make_async_remote_copy(
            src_ref=pats.at[t], dst_ref=pats.at[t], send_sem=pat_send.at[d], recv_sem=pat_recv.at[t],
            device_id=(c, lax.rem(t + d, TM)), device_id_type=MESH,
        )

    def send_pattern(d, _):
        pat_copy(d).start()
        return 0

    lax.fori_loop(1, TM, send_pattern, 0)

    acc[...] = jnp.zeros_like(acc)

    wide = jnp.concatenate([taps[...], jnp.zeros((1, 192), jnp.float32)], 1)
    band = pltpu.roll(jnp.broadcast_to(wide, (128, 256)), 0, 1, stride=1, stride_axis=0)[:, 0:192]
    inner = lax.broadcasted_iota(jnp.int32, (768, 256), 0)
    outer = lax.broadcasted_iota(jnp.int32, (768, 256), 1)
    boxcar = jnp.where((inner >= outer) & (inner <= outer + 512), 1.0, 0.0).astype(jnp.bfloat16)

    def await_halo(sides):
        for e, (dc, dt) in enumerate(DIRS):
            if (dt != 0) == sides:
                @pl.when(inside(-dc, -dt))
                def _():
                    halo(e, dc, dt, -1).wait_recv()

    await_halo(False)

    def clean(b):
        cols = pl.ds(pl.multiple_of(256 * b, 256), 256)
        f = lively * jnp.dot(
            band, rim[:, cols], precision=lax.Precision.HIGHEST, preferred_element_type=jnp.float32
        )
        filtered[:, cols] = f
        rest = jnp.abs(f)
        for part in range(3):
            sizes[part, :, cols] = rest.astype(jnp.bfloat16)
            rest = rest - sizes[part, :, cols].astype(jnp.float32)

    def scale(b):
        first = pl.multiple_of(256 * b, 256)
        total = None
        for part in range(3):
            s = jnp.dot(sizes[part, :, pl.ds(first, 768)], boxcar, preferred_element_type=jnp.float32)
            total = s if total is None else total + s
        level = total / (2 * HALF_WIN + 1)
        mine = filtered[:, pl.ds(first + 256, 256)]
        nbuf[0:128, pl.ds(first, 256)] = (mine / (level + 1e-5)).astype(jnp.bfloat16)

    def up(piece):
        cols = pl.ds(*((256, 512), (0, 256), (768, 256))[piece])
        return pltpu.make_async_remote_copy(
            src_ref=nbuf.at[pl.ds(0, 48), cols], dst_ref=nbuf.at[pl.ds(128, 48), cols],
            send_sem=up_send.at[piece], recv_sem=up_recv.at[piece], device_id=(c - 1, t), device_id_type=MESH,
        )

    def up_start(piece):
        @pl.when(c > 0)
        def _():
            up(piece).start()

    turns = [(1, 1), (1, 2), (1, 3), (1, 4), (0, 1), (0, 2), (1, 0), (1, 5), (0, 0), (0, 3)]

    def turn(n, _):
        block = pick([b for _, b in turns], n)
        cleans = pick([k for k, _ in turns], n)

        @pl.when(n == 6)
        def _():
            up_start(0)
            await_halo(True)

        @pl.when(cleans == 1)
        def _():
            clean(block)

        @pl.when(cleans == 0)
        def _():
            scale(block)

        return 0

    lax.fori_loop(0, len(turns), turn, 0)

    up_start(1)
    up_start(2)

    def other(r):
        dx, dy = pick([d[0] for d in ORDER], r), pick([d[1] for d in ORDER], r)
        return lax.rem(t // 4 + dx, 2) * 4 + lax.rem(lax.rem(t, 4) + 4 - dy, 4)

    def source(r):
        dx, dy = pick([d[0] for d in ORDER], r), pick([d[1] for d in ORDER], r)
        return lax.rem(t // 4 + dx, 2) * 4 + lax.rem(lax.rem(t, 4) + dy, 4)

    def fill(dest, to):
        first = pl.multiple_of(dest * 16, 16)
        offsets = [jnp.concatenate([pats[dest, 8 * k : 8 * k + 8, :]] * 2, 0) for k in range(PAIRS)]
        for j in range(8):
            cols = slice(128 * j, 128 * j + 128)
            blocks = [nbuf[pl.ds(pl.multiple_of(first + 16 * o, 16), 16), cols] for o in range(4)]
            to[0:16, cols] = blocks[0]
            blocks = [block.astype(jnp.float32) for block in blocks]
            for k in range(PAIRS):
                chosen = blocks[0]
                for o in range(1, 4):
                    chosen = jnp.where(offsets[k] == o, blocks[o], chosen)
                to[16 * k + 16 : 16 * k + 32, cols] = chosen.astype(jnp.bfloat16)

    def deliver(r, dest):
        return pltpu.make_async_remote_copy(
            src_ref=pack.at[r], dst_ref=slots.at[t + 1], send_sem=send_sem.at[r], recv_sem=recv_sem.at[t],
            device_id=(c, dest), device_id_type=MESH,
        )

    def arrival(r):
        src = source(r)
        return pltpu.make_async_remote_copy(
            src_ref=pack.at[r], dst_ref=slots.at[src + 1], send_sem=send_sem.at[r], recv_sem=recv_sem.at[src],
            device_id=(c, src), device_id_type=MESH,
        )

    def await_pattern(d, _):
        src = lax.rem(t + d, TM)
        pltpu.make_async_remote_copy(
            src_ref=pats.at[src], dst_ref=pats.at[src], send_sem=pat_send.at[d], recv_sem=pat_recv.at[src],
            device_id=(c, src), device_id_type=MESH,
        ).wait_recv()
        return 0

    lax.fori_loop(1, TM, await_pattern, 0)

    def hand_out(n, _):
        r = lax.rem(n + 1, TM)
        dest = other(r)

        @pl.when((n == TM) & (c < chans - 1))
        def _():
            for piece in range(3):
                up(piece).wait_recv()

        @pl.when((dest >= 5) == (n >= TM))
        def _():
            fill(dest, pack.at[r])

            @pl.when(r > 0)
            def _():
                deliver(r, dest).start()

            @pl.when(r == 0)
            def _():
                slots[t + 1] = pack[0]

        return 0

    lax.fori_loop(0, 2 * TM, hand_out, 0)

    def follow(done, r):
        deliver(done, other(done)).wait_send()
        deliver(r, other(r)).start()

    steps, needs = schedule()

    def step(n, _):
        def take(r, _):
            arrival(r).wait_recv()
            return 0

        begin = jnp.where(n == 0, 0, look_up(needs, t, jnp.maximum(n - 1, 0)))
        lax.fori_loop(begin + 1, look_up(needs, t, n) + 1, take, 0)
        low = look_up(steps, t, n)
        accumulate(slots.at[low], slots.at[low + 1], acc, own, near, far)
        return 0

    lax.fori_loop(0, TM + 1, step, 0)

    def put(qh):
        cols = pl.ds(pl.multiple_of(128 * qh, 128), 128)
        return pltpu.make_async_copy(out.at[:, :, :, cols], final.at[:, :, :, cols], out_sem.at[qh])

    def turn_over(qh, _):
        transpose(acc, out, qh, 0)
        put(qh).start()
        return 0

    def written(qh, _):
        put(qh).wait()
        return 0

    lax.fori_loop(0, 8, turn_over, 0)

    def finish(r, _):
        deliver(r, other(r)).wait_send()

        pat_copy(r).wait_send()
        return 0

    lax.fori_loop(1, TM, finish, 0)
    for e, (dc, dt) in enumerate(DIRS):
        @pl.when(inside(dc, dt))
        def _():
            halo(e, dc, dt).wait_send()

    @pl.when(c > 0)
    def _():
        for piece in range(3):
            up(piece).wait_send()

    lax.fori_loop(0, 8, written, 0)


def front(record, alive, taps, pattern):
    dma = pltpu.SemaphoreType.DMA
    return pl.pallas_call(
        front_kernel,
        out_shape=jax.ShapeDtypeStruct((PAIRS, BLOCK, BLOCK, 2 * LAG), jnp.float32),
        in_specs=[pl.BlockSpec(memory_space=pltpu.HBM)] * 4,
        out_specs=pl.BlockSpec(memory_space=pl.ANY),
        scratch_shapes=[
            pltpu.VMEM((8, 256, 256), jnp.float32),
            pltpu.VMEM((PAIRS, BLOCK, BLOCK, 2 * LAG), jnp.float32),
            pltpu.VMEM((128, 1024), jnp.float32),
            pltpu.VMEM((1, 128), jnp.int32),
            pltpu.VMEM((1, 64), jnp.float32),
            pltpu.SMEM((1, 2), jnp.int32),
            pltpu.VMEM((192, 1536), jnp.float32),
            pltpu.VMEM((176, 1024), jnp.bfloat16),
            pltpu.VMEM((TM, 48, 1024), jnp.bfloat16),
            pltpu.VMEM((TM, 16, 128), jnp.int32),
            pltpu.VMEM((TM + 2, 48, 1024), jnp.bfloat16),
            pltpu.VMEM((256, 1024), jnp.bfloat16),
            pltpu.VMEM((16, 1152), jnp.float32),
            pltpu.VMEM((256, 1920), jnp.bfloat16),
            pltpu.VMEM((128, 1536), jnp.float32),
            pltpu.VMEM((3, 128, 1536), jnp.bfloat16),
            dma((8,)), dma((4,)), dma((8,)), dma((8,)), dma((TM,)), dma((TM,)), dma((3,)), dma((3,)), dma((TM,)), dma((TM,)),
        ],
        compiler_params=pltpu.CompilerParams(
            collective_id=0, has_side_effects=True, vmem_limit_bytes=60 << 20
        ),
        name="front",
    )(record, alive.reshape(1, 128), taps.reshape(1, 64), pattern)


def body(record, alive, taps, pattern):
    return front(record, alive, taps, pattern)[None] * (1.0 / math.sqrt(T))


def solution(mesh):
    placed = (P("chan", "tm"), P("chan"), P(), P(("chan", "tm"), None))
    return jax.shard_map(
        body,
        mesh=mesh,
        in_specs=placed,
        out_specs=P(("chan", "tm"), None, None, None, None),
        check_vma=False,
    )
```
